512 devices in a mesh: replica: 32 (over z, y_hi), tensor: 16 (over y_lo, x, core).
Axes of the slice: x: 4, y: 8 (y_hi: 4, y_lo: 2; y = y_hi * 2 + y_lo), z: 8, core: 2. Of those that a mesh axis runs over, the one named last changes fastest.
Arguments:
- pseudo_grad: bfloat16 [32, 8192, 512], P('replica', 'tensor'), may hold values from -0.1796875 to 0.1796875
- stale_avg: bfloat16 [8192, 512], P('tensor'), may hold values from -0.011962891 to 0.011962891
- momentum: float32 [16, 32, 16, 512], P('tensor', 'replica'), may hold values from -0.012 to 0.012
- weight: bfloat16 [8192, 512], P('tensor'), may hold values from -0.0625 to 0.0625
- tokens: bfloat16 [32768, 8192], P('replica', 'tensor'), may hold values from -6 to 6
- cotangent: bfloat16 [32768, 512], P(('replica', 'tensor')), may hold values from -6 to 6
Outputs:
- avg_codes: float32 [16, 32, 16, 512], P('tensor', 'replica')
- avg_scales: float32 [16, 32, 16, 4], P('tensor', 'replica')
- new_momentum: float32 [16, 32, 16, 512], P('tensor', 'replica')
- new_weight: bfloat16 [32, 8192, 512], P('replica', 'tensor')
- keys: bfloat16 [32768, 512], P(('replica', 'tensor'))
- grad_tokens: bfloat16 [32768, 8192], P('replica', 'tensor')
- grad_weight: bfloat16 [32, 8192, 512], P('replica', 'tensor')
The draws below stay inside these ranges and needn't reach their ends.
All inputs are finite; a program needn't handle non-finite values. Where the reference program divides by a largest or mean magnitude, that divisor is 1e-20 or more.
Results may differ from the reference program's by a relative error of at most 0.0018.
Values may be sent and summed in bfloat16 or wider, within the bound.
No kernel may reach another device: no remote copies, remote signals or barrier semaphores. Data moves between devices by JAX's collectives and lax.ppermute only.
A program may use at most 64 MiB of HBM per device.

```python
import jax
import jax.numpy as jnp
from jax import lax

D = 8192
KV_WIDTH = 512
BLOCK = 128
TOK_DEV = 1024
ROWS = 32768
OWN = 16
NBLOCKS = 4
N_REPLICA = 32
N_TENSOR = 16


def raised(array, rng, source, target, blocks, factor):
    def block_of(dim):
        return (jnp.arange(array.shape[dim]) // (array.shape[dim] // blocks)).reshape((-1,) + (1,) * (array.ndim - 1 - dim))

    one_side = jax.random.permutation(rng, blocks)[block_of(target)]
    other_side = (block_of(target) + blocks // 2) % blocks
    return jnp.where((block_of(source) == one_side) | (block_of(source) == other_side), factor * array, array)


def steps_of(stream_key, shape, shards, least, largest):
    level = 1.0
    for axis_at, shards_of in shards:
        heights = jax.random.uniform(jax.random.fold_in(jax.random.fold_in(stream_key, 6), axis_at), (shards_of,), jnp.float32, least / len(shards), largest / len(shards))
        level = level * jnp.repeat(jnp.exp(heights), shape[axis_at] // shards_of).reshape((-1,) + (1,) * (len(shape) - 1 - axis_at))
    return level


def normal_values(key, shape, width, bound, cuts=(), dtype=jnp.bfloat16):
    values = jax.random.normal(key, shape, jnp.float32) * width
    if len(cuts) > 0:
        values = steps_of(key, shape, cuts, -0.22, 0.18) * values
    return jnp.clip(values, min=-bound, max=bound).astype(dtype)


def heavy_noise(rng, shape, width, limit, shards, heavy, kind=jnp.bfloat16):
    array = width * jax.random.normal(rng, shape, jnp.float32)
    if shards:
        array = array * steps_of(rng, shape, shards, -0.22, 0.18)
    return jnp.clip(raised(array, jax.random.fold_in(rng, 3), *heavy), -limit, limit).astype(kind)


def setup_inputs(seed: int = 0) -> dict:
    seeds = jax.random.split(jax.random.key(seed), 7)
    return {
        "pseudo_grad": heavy_noise(seeds[0], (N_REPLICA, D, KV_WIDTH), 0.03, 0.1796875, ((0, 32), (1, 16)), (0, 1, 32, 2.75)),
        "stale_avg": normal_values(seeds[1], (D, KV_WIDTH), 0.002, 0.011962891, ((0, 16),)),
        "momentum": normal_values(seeds[2], (N_TENSOR, N_REPLICA, OWN, KV_WIDTH), 0.002, 0.012, ((0, 16), (1, 32)), jnp.float32),
        "weight": normal_values(seeds[3], (D, KV_WIDTH), D ** -0.5, 0.0625, ((0, 16),)),
        "tokens": normal_values(seeds[4], (ROWS, D), 1.0, 6.0, ((0, 32), (1, 16))),
        "cotangent": normal_values(seeds[5], (ROWS, KV_WIDTH), 1.0, 6.0, ((0, 512),)),
    }


OUTER_RATE = 0.7
MOMENTUM_COEF = 0.9
EPSILON = 1e-06

def reference(pseudo_grad, stale_avg, momentum, weight, tokens, cotangent):

    def accumulate(index, acc):
        return acc + pseudo_grad[index].astype(jnp.float32)
    total = lax.fori_loop(0, N_REPLICA, accumulate, jnp.zeros((D, KV_WIDTH), jnp.float32))
    average = total / N_REPLICA
    blocks = average.reshape(D, NBLOCKS, BLOCK)
    scales = lax.optimization_barrier(jnp.max(jnp.abs(blocks), axis=-1)) + EPSILON
    normalized = (blocks / scales[:, :, None]).reshape(D, KV_WIDTH)
    avg_codes = normalized.reshape(N_TENSOR, N_REPLICA, OWN, KV_WIDTH)
    avg_scales = scales.reshape(N_TENSOR, N_REPLICA, OWN, NBLOCKS)
    stale_full = stale_avg.astype(jnp.float32)
    moment_next = MOMENTUM_COEF * momentum.reshape(D, KV_WIDTH) + stale_full
    outer_step = (stale_full + MOMENTUM_COEF * moment_next).astype(jnp.bfloat16)
    outer_step = lax.optimization_barrier(outer_step).astype(jnp.float32)
    weight_full = weight.astype(jnp.float32)

    def update_one(delta):
        change = outer_step + (delta.astype(jnp.float32) - stale_full) / N_REPLICA
        return (weight_full - OUTER_RATE * change).astype(jnp.bfloat16)
    new_weight = lax.map(update_one, pseudo_grad)
    new_momentum = moment_next.reshape(N_TENSOR, N_REPLICA, OWN, KV_WIDTH)
    keys = jnp.dot(tokens, weight, preferred_element_type=jnp.float32).astype(jnp.bfloat16)
    grad_tokens = jnp.dot(cotangent, weight.T, preferred_element_type=jnp.float32).astype(jnp.bfloat16)
    token_groups = tokens.reshape(N_REPLICA, TOK_DEV, D)
    cot_groups = cotangent.reshape(N_REPLICA, TOK_DEV, KV_WIDTH)

    def weight_grad(pair):
        return jnp.dot(pair[0].T, pair[1], preferred_element_type=jnp.float32).astype(jnp.bfloat16)
    grad_weight = lax.map(weight_grad, (token_groups, cot_groups))
    return (avg_codes, avg_scales, new_momentum, new_weight, keys, grad_tokens, grad_weight)
```

```python
import functools

import jax
import jax.numpy as jnp
from jax import lax
from jax.experimental import pallas as pl
from jax.experimental.pallas import tpu as pltpu
from jax.sharding import Mesh, PartitionSpec as P

BLOCK = 128
OUTER_RATE = 0.7
MOMENTUM_COEF = 0.9
EPSILON = 1e-06

REPLICA = ("z", "yh")
TENSOR = ("yl", "x", "core")
CHIPS = ("yl", "x")
SIZES = (8, 4, 2, 4, 2)

EST_PREPARE = 1.0
EST_OWN = 1.0
EST_TAIL = 5.0
EST_GRADS = 1.0

VMEM = pl.BlockSpec(memory_space=pltpu.VMEM)
SMEM = pl.BlockSpec(memory_space=pltpu.SMEM)


def call(kernel, out_shape, ins, us, scratch=()):
    return pl.pallas_call(
        kernel,
        out_shape=out_shape,
        in_specs=ins,
        out_specs=jax.tree.map(lambda _: VMEM, out_shape),
        scratch_shapes=list(scratch),
        compiler_params=pltpu.CompilerParams(vmem_limit_bytes=24 * 1024 * 1024),
        cost_estimate=pl.CostEstimate(
            flops=0, bytes_accessed=int(us * 3.69e6), transcendentals=0
        ),
    )


def prepare_kernel(at, grads, stale, momentum, sent, moment_next):
    owned = momentum.shape[0]
    rows = stale[pl.ds(pl.multiple_of(at[0] * owned, owned), owned), :].astype(jnp.float32)
    moment = MOMENTUM_COEF * momentum[...] + rows
    moment_next[...] = moment
    step = (rows + MOMENTUM_COEF * moment).astype(jnp.bfloat16)
    sent[:, :owned, :] = grads[...]
    sent[:, owned:, :] = jnp.broadcast_to(step[None], grads.shape)


def own_kernel(at, tokens, weight, arrived, kept, *rest):
    outs, held = rest[:-1], rest[-1]
    chips, _, mine, width = tokens.shape
    rows = tokens[:, at[1]].reshape(chips * mine, width)
    part = jnp.dot(rows, weight[...], preferred_element_type=jnp.float32) + arrived[...]
    held[...] = part.reshape(held.shape)
    line = held.shape[1]
    kept[...] = held[:, at[2]]
    for k, out in enumerate(outs):
        out[...] = held[:, lax.rem(at[2] + k + 1, line)]


def grads_kernel(at, tokens, weight, cot_mine, cot_theirs, grad_tokens, grad_weight, held):
    chips, cores, mine, width = held.shape
    held[:, at[1]] = cot_mine[...]
    held[:, 1 - at[1]] = cot_theirs[...]
    cot = held[...].reshape(chips * cores * mine, width)
    grad_tokens[...] = lax.dot_general(
        cot, weight[...], (((1,), (1,)), ((), ())), preferred_element_type=jnp.float32
    ).astype(jnp.bfloat16)
    grad_weight[...] = lax.dot_general(
        tokens[...], cot, (((0,), (0,)), ((), ())), preferred_element_type=jnp.float32
    ).astype(jnp.bfloat16)


def tail_kernel(got, grads, stale, weight, codes, scales, new_weight):
    replicas, twice, width = got.shape
    owned = twice // 2
    total = jnp.sum(got[:, :owned, :].astype(jnp.float32), axis=0)
    average = total / replicas
    parts, largest = [], []
    for b in range(width // BLOCK):
        block = average[:, b * BLOCK:(b + 1) * BLOCK]
        scale = jnp.max(jnp.abs(block), axis=-1, keepdims=True) + EPSILON
        parts.append(block / scale)
        largest.append(scale)
    codes[...] = jnp.concatenate(parts, axis=1)
    scales[...] = jnp.concatenate(largest, axis=1)
    change = got[:, owned:, :].astype(jnp.float32) + (
        grads[...].astype(jnp.float32) - stale[...].astype(jnp.float32)
    ) / replicas
    new_weight[...] = (weight[...].astype(jnp.float32) - OUTER_RATE * change).astype(jnp.bfloat16)


def shift(value, axis, k):
    n = lax.axis_size(axis)
    return lax.ppermute(value, axis, [(i, (i + k) % n) for i in range(n)])


def pick(value, index, axis):
    return lax.dynamic_index_in_dim(value, index, axis, False)


def body(pseudo_grad, stale_avg, momentum, weight, tokens, cotangent):
    replicas = lax.axis_size("z") * lax.axis_size("yh")
    runs, line = lax.axis_size("yl"), lax.axis_size("x")
    chips = runs * line
    core, x_at, yl_at = lax.axis_index("core"), lax.axis_index("x"), lax.axis_index("yl")
    at = jnp.stack([lax.axis_index(REPLICA), core, x_at, yl_at]).astype(jnp.int32)
    owned = momentum.shape[2]
    width = weight.shape[1]
    nblocks = width // BLOCK
    mine = cotangent.shape[0]
    f32, bf16 = jnp.float32, jnp.bfloat16
    struct = jax.ShapeDtypeStruct

    cot_mine = lax.all_to_all(
        jnp.broadcast_to(cotangent[None], (chips, mine, width)), CHIPS, 0, 0
    )

    grouped = tokens.reshape(chips, 2, mine, tokens.shape[1])
    rows_theirs = pick(grouped, 1 - core, 1).reshape(chips * mine, -1)
    arrived = shift(jnp.dot(rows_theirs, weight, preferred_element_type=f32), "core", 1)

    grads = pseudo_grad[0].reshape(replicas, owned, width)
    sent, moment_next = call(
        prepare_kernel,
        [struct((replicas, 2 * owned, width), bf16), struct((owned, width), f32)],
        [SMEM, VMEM, VMEM, VMEM],
        EST_PREPARE,
    )(at, grads, stale_avg, momentum[0, 0])
    got = lax.all_to_all(sent, REPLICA, 0, 0)

    arrived, cot_mine = lax.optimization_barrier((arrived, cot_mine))
    piece = struct((runs, mine, width), f32)
    kept, *pieces = call(
        own_kernel,
        [piece] * line,
        [SMEM, VMEM, VMEM, VMEM],
        EST_OWN,
        [pltpu.VMEM((runs, line, mine, width), f32)],
    )(at, grouped, weight, arrived)
    from_x = [shift(pieces[k - 1], "x", k) for k in (2, 1, 3)]

    cot_theirs = shift(cot_mine, "core", 1)
    grad_tokens, grad_weight = call(
        grads_kernel,
        [struct(tokens.shape, bf16), struct((tokens.shape[1], width), bf16)],
        [SMEM] + [VMEM] * 4,
        EST_GRADS,
        [pltpu.VMEM(grouped.shape, bf16)],
    )(at, tokens, weight, cot_mine, cot_theirs)

    from_x, grad_weight, grad_tokens = lax.optimization_barrier((from_x, grad_weight, grad_tokens))
    acc = kept + from_x[0] + from_x[1] + from_x[2]
    keys = (pick(acc, yl_at, 0) + shift(pick(acc, 1 - yl_at, 0), "yl", 1)).astype(bf16)

    codes, scales, new_weight = call(
        tail_kernel,
        [struct((owned, width), f32), struct((owned, nblocks), f32), struct((replicas, owned, width), bf16)],
        [VMEM] * 4,
        EST_TAIL,
    )(got, grads, stale_avg.reshape(grads.shape), weight.reshape(grads.shape))
    return (
        codes[None, None],
        scales[None, None],
        moment_next[None, None],
        new_weight.reshape(pseudo_grad.shape),
        keys,
        grad_tokens,
        grad_weight[None],
    )


def solution(mesh):
    fine = Mesh(mesh.devices.reshape(SIZES), REPLICA + TENSOR)
    return jax.shard_map(
        body,
        mesh=fine,
        in_specs=(
            P(REPLICA, TENSOR, None),
            P(TENSOR, None),
            P(TENSOR, REPLICA, None, None),
            P(TENSOR, None),
            P(REPLICA, TENSOR),
            P(REPLICA + TENSOR, None),
        ),
        out_specs=(
            P(TENSOR, REPLICA, None, None),
            P(TENSOR, REPLICA, None, None),
            P(TENSOR, REPLICA, None, None),
            P(REPLICA, TENSOR, None),
            P(REPLICA + TENSOR, None),
            P(REPLICA, TENSOR),
            P(REPLICA, TENSOR, None),
        ),
        check_vma=False,
    )
```

```python
import jax
import jax.numpy as jnp
from jax import lax
from jax.experimental import pallas as pl
from jax.experimental.pallas import tpu as pltpu
from jax.sharding import Mesh, PartitionSpec as P

BLOCK = 128
OUTER_RATE = 0.7
MOMENTUM_COEF = 0.9
EPSILON = 1e-06

REPLICA = ("z", "yh")
TENSOR = ("yl", "x", "core")
CHIPS = ("yl", "x")
SIZES = (8, 4, 2, 4, 2)

MIB = 1024 * 1024
VMEM = pl.BlockSpec(memory_space=pltpu.VMEM)
SMEM = pl.BlockSpec(memory_space=pltpu.SMEM)
HBM = pl.BlockSpec(memory_space=pltpu.HBM)
F32, BF16 = jnp.float32, jnp.bfloat16
struct = jax.ShapeDtypeStruct


def call(kernel, ins, outs, moved, flops, scratch=(), limit=8 * MIB):
    return pl.pallas_call(
        kernel,
        out_shape=[struct(shape, dtype) for shape, dtype, _ in outs],
        in_specs=ins,
        out_specs=[spec for _, _, spec in outs],
        scratch_shapes=list(scratch),
        compiler_params=pltpu.CompilerParams(vmem_limit_bytes=limit),
        cost_estimate=pl.CostEstimate(flops=flops, bytes_accessed=moved, transcendentals=0),
    )


def spread_kernel(rows, out, sems):
    copies = [pltpu.make_async_copy(rows, out.at[i], sems.at[i]) for i in range(out.shape[0])]
    for copy in copies:
        copy.start()
    for copy in copies:
        copy.wait()


def front_kernel(at, grads, stale, momentum, tokens, weight, sent, moment_next, theirs, rows, step, other, sems):
    owned = momentum.shape[0]
    chips, mine, width = other.shape
    copy_rows = pltpu.make_async_copy(
        stale.at[pl.ds(pl.multiple_of(at[0] * owned, owned), owned), :], rows, sems.at[0]
    )
    copy_tokens = pltpu.make_async_copy(tokens.at[:, 1 - at[1]], other, sems.at[1])
    copy_grads = pltpu.make_async_copy(grads, sent.at[:, :owned, :], sems.at[2])
    copy_step = pltpu.make_async_copy(step, sent.at[:, owned:, :], sems.at[3])
    copy_rows.start()
    copy_tokens.start()
    copy_grads.start()
    copy_rows.wait()
    old = rows[...].astype(F32)
    moment = MOMENTUM_COEF * momentum[...] + old
    moment_next[...] = moment
    step[...] = jnp.broadcast_to((old + MOMENTUM_COEF * moment).astype(BF16)[None], step.shape)
    copy_step.start()
    copy_tokens.wait()
    theirs[...] = jnp.dot(
        other[...].reshape(chips * mine, width), weight[...], preferred_element_type=F32
    )
    copy_grads.wait()
    copy_step.wait()


def own_kernel(at, tokens, weight, arrived, *outs):
    runs, mine, width = outs[0].shape
    line = len(outs)
    for k, out in enumerate(outs):
        x = lax.rem(at[2] + k, line)
        rows = jnp.concatenate([tokens[y * line + x, at[1]] for y in range(runs)], axis=0)
        part = jnp.dot(rows, weight[...], preferred_element_type=F32)
        for y in range(runs):
            out[y] = part[y * mine:(y + 1) * mine] + arrived[y * line + x]


def grads_kernel(at, tokens, weight, cot_mine, cot_theirs, grad_tokens, grad_weight, held, sems):
    chips, cores, mine, width = held.shape
    copies = [
        pltpu.make_async_copy(cot_mine, held.at[:, at[1]], sems.at[0]),
        pltpu.make_async_copy(cot_theirs, held.at[:, 1 - at[1]], sems.at[1]),
    ]
    for copy in copies:
        copy.start()
    for copy in copies:
        copy.wait()
    cot = held[...].reshape(chips * cores * mine, width)
    grad_tokens[...] = lax.dot_general(
        cot, weight[...], (((1,), (1,)), ((), ())), preferred_element_type=F32
    ).astype(BF16)
    grad_weight[...] = lax.dot_general(
        tokens[...], cot, (((0,), (0,)), ((), ())), preferred_element_type=F32
    ).astype(BF16)


def tail_kernel(got, grads, stale, weight, here, there, codes, scales, new_weight, keys):
    replicas, twice, width = got.shape
    owned = twice // 2
    total = jnp.sum(got[:, :owned, :].astype(F32), axis=0)
    average = total / replicas
    diagonal = lax.broadcasted_iota(jnp.int32, (owned, owned), 0) == lax.broadcasted_iota(
        jnp.int32, (owned, owned), 1
    )
    for b in range(width // BLOCK):
        columns = slice(b * BLOCK, (b + 1) * BLOCK)
        block = average[:, columns]
        scale = jnp.max(jnp.abs(block), axis=-1, keepdims=True) + EPSILON
        codes[:, columns] = block / scale
        scales[b:b + 1, :] = jnp.sum(jnp.where(diagonal, scale, 0.0), axis=0, keepdims=True)
    change = got[:, owned:, :].astype(F32) + (grads[...].astype(F32) - stale[...].astype(F32)) / replicas
    new_weight[...] = (weight[...].astype(F32) - OUTER_RATE * change).astype(BF16)
    keys[...] = (here[...] + there[...]).astype(BF16)


def shift(value, axis, k):
    n = lax.axis_size(axis)
    return lax.ppermute(value, axis, [(i, (i + k) % n) for i in range(n)])


def pick(value, index, axis):
    return lax.dynamic_index_in_dim(value, index, axis, False)


def body(pseudo_grad, stale_avg, momentum, weight, tokens, cotangent):
    replicas = lax.axis_size("z") * lax.axis_size("yh")
    runs, line = lax.axis_size("yl"), lax.axis_size("x")
    chips = runs * line
    core, x_at, yl_at = lax.axis_index("core"), lax.axis_index("x"), lax.axis_index("yl")
    at = jnp.stack([lax.axis_index(REPLICA), core, x_at, yl_at]).astype(jnp.int32)
    owned = momentum.shape[2]
    rows, width = weight.shape
    nblocks = width // BLOCK
    mine = cotangent.shape[0]
    dma = pltpu.SemaphoreType.DMA
    block = rows * width

    (copies,) = call(
        spread_kernel,
        [VMEM],
        [((chips, mine, width), BF16, HBM)],
        4 * cotangent.size * chips,
        0,
        [dma((chips,))],
    )(cotangent)
    cot_mine = lax.all_to_all(copies, CHIPS, 0, 0)

    grads = pseudo_grad[0].reshape(replicas, owned, width)
    grouped = tokens.reshape(chips, 2, mine, rows)
    sent, moment_next, theirs = call(
        front_kernel,
        [SMEM, HBM, HBM, VMEM, HBM, VMEM],
        [
            ((replicas, 2 * owned, width), BF16, HBM),
            ((owned, width), F32, VMEM),
            ((chips * mine, width), F32, VMEM),
        ],
        12 * block,
        0,
        [
            pltpu.VMEM((owned, width), BF16),
            pltpu.VMEM((replicas, owned, width), BF16),
            pltpu.VMEM((chips, mine, rows), BF16),
            dma((4,)),
        ],
    )(at, grads, stale_avg, momentum[0, 0], grouped, weight)
    arrived = shift(theirs, "core", 1).reshape(chips, mine, width)
    got = lax.all_to_all(sent, REPLICA, 0, 0)

    arrived, cot_mine = lax.optimization_barrier((arrived, cot_mine))
    kept, *pieces = call(
        own_kernel,
        [SMEM, VMEM, VMEM, VMEM],
        [((runs, mine, width), F32, VMEM)] * line,
        10 * block,
        0,
    )(at, grouped, weight, arrived)
    from_x = [shift(pieces[k - 1], "x", k) for k in (2, 1, 3)]

    cot_theirs = shift(cot_mine, "core", 1)
    grad_tokens, grad_weight = call(
        grads_kernel,
        [SMEM, VMEM, VMEM, HBM, HBM],
        [(tokens.shape, BF16, VMEM), ((rows, width), BF16, VMEM)],
        12 * block,
        0,
        [pltpu.VMEM(grouped.shape, BF16), dma((2,))],
        16 * MIB,
    )(at, tokens, weight, cot_mine, cot_theirs)

    from_x, grad_weight, grad_tokens = lax.optimization_barrier((from_x, grad_weight, grad_tokens))
    acc = kept + from_x[0] + from_x[1] + from_x[2]
    there = shift(pick(acc, 1 - yl_at, 0), "yl", 1)

    codes, scales, new_weight, keys = call(
        tail_kernel,
        [VMEM] * 6,
        [
            ((owned, width), F32, VMEM),
            ((nblocks, owned), F32, VMEM),
            ((replicas, owned, width), BF16, VMEM),
            ((mine, width), BF16, VMEM),
        ],
        12 * block,
        0,
        limit=12 * MIB,
    )(got, grads, stale_avg.reshape(grads.shape), weight.reshape(grads.shape), pick(acc, yl_at, 0), there)
    return (
        codes[None, None],
        scales.T[None, None],
        moment_next[None, None],
        new_weight.reshape(pseudo_grad.shape),
        keys,
        grad_tokens,
        grad_weight[None],
    )


def solution(mesh):
    fine = Mesh(mesh.devices.reshape(SIZES), REPLICA + TENSOR)
    return jax.shard_map(
        body,
        mesh=fine,
        in_specs=(
            P(REPLICA, TENSOR, None),
            P(TENSOR, None),
            P(TENSOR, REPLICA, None, None),
            P(TENSOR, None),
            P(REPLICA, TENSOR),
            P(REPLICA + TENSOR, None),
        ),
        out_specs=(
            P(TENSOR, REPLICA, None, None),
            P(TENSOR, REPLICA, None, None),
            P(TENSOR, REPLICA, None, None),
            P(REPLICA, TENSOR, None),
            P(REPLICA + TENSOR, None),
            P(REPLICA, TENSOR),
            P(REPLICA, TENSOR, None),
        ),
        check_vma=False,
    )
```

```python
import jax
import jax.numpy as jnp
from jax import lax
from jax.experimental import pallas as pl
from jax.experimental.pallas import tpu as pltpu
from jax.sharding import Mesh, PartitionSpec as P

BLOCK = 128
OUTER_RATE = 0.7
MOMENTUM_COEF = 0.9
EPSILON = 1e-06

REPLICA = ("z", "yh")
TENSOR = ("yl", "x", "core")
CHIPS = ("yl", "x")
SIZES = (8, 4, 2, 4, 2)

MIB = 1024 * 1024
VMEM = pl.BlockSpec(memory_space=pltpu.VMEM)
SMEM = pl.BlockSpec(memory_space=pltpu.SMEM)
HBM = pl.BlockSpec(memory_space=pltpu.HBM)
F32, BF16 = jnp.float32, jnp.bfloat16
struct = jax.ShapeDtypeStruct


def call(kernel, ins, outs, moved, flops, scratch=(), limit=8 * MIB):
    return pl.pallas_call(
        kernel,
        out_shape=[struct(shape, dtype) for shape, dtype, _ in outs],
        in_specs=ins,
        out_specs=[spec for _, _, spec in outs],
        scratch_shapes=list(scratch),
        compiler_params=pltpu.CompilerParams(vmem_limit_bytes=limit),
        cost_estimate=pl.CostEstimate(flops=flops, bytes_accessed=moved, transcendentals=0),
    )


def spread_kernel(rows, out, sems):
    copies = [pltpu.make_async_copy(rows, out.at[i], sems.at[i]) for i in range(out.shape[0])]
    for copy in copies:
        copy.start()
    for copy in copies:
        copy.wait()


def front_kernel(at, grads, stale, momentum, tokens, weight, sent, moment_next, theirs, rows, step, other, sems):
    owned = momentum.shape[0]
    chips, mine, width = other.shape
    copy_rows = pltpu.make_async_copy(
        stale.at[pl.ds(pl.multiple_of(at[0] * owned, owned), owned), :], rows, sems.at[0]
    )
    copy_tokens = pltpu.make_async_copy(tokens.at[:, 1 - at[1]], other, sems.at[1])
    copy_grads = pltpu.make_async_copy(grads, sent.at[:, :owned, :], sems.at[2])
    copy_step = pltpu.make_async_copy(step, sent.at[:, owned:, :], sems.at[3])
    copy_rows.start()
    copy_tokens.start()
    copy_grads.start()
    copy_rows.wait()
    old = rows[...].astype(F32)
    moment = MOMENTUM_COEF * momentum[...] + old
    moment_next[...] = moment
    step[...] = jnp.broadcast_to((old + MOMENTUM_COEF * moment).astype(BF16)[None], step.shape)
    copy_step.start()
    copy_tokens.wait()
    theirs[...] = jnp.dot(
        other[...].reshape(chips * mine, width), weight[...], preferred_element_type=F32
    )
    copy_grads.wait()
    copy_step.wait()


def own_kernel(at, tokens, weight, arrived, *outs):
    runs, mine, width = outs[0].shape
    line = len(outs)
    for k, out in enumerate(outs):
        x = lax.rem(at[2] + k, line)
        rows = jnp.concatenate([tokens[y * line + x, at[1]] for y in range(runs)], axis=0)
        part = jnp.dot(rows, weight[...], preferred_element_type=F32)
        for y in range(runs):
            out[y] = part[y * mine:(y + 1) * mine] + arrived[y * line + x]


def grads_kernel(at, tokens, weight, cot_mine, cot_theirs, grad_tokens, grad_weight, held, sems):
    chips, cores, mine, width = held.shape
    copies = [
        pltpu.make_async_copy(cot_mine, held.at[:, at[1]], sems.at[0]),
        pltpu.make_async_copy(cot_theirs, held.at[:, 1 - at[1]], sems.at[1]),
    ]
    for copy in copies:
        copy.start()
    for copy in copies:
        copy.wait()
    cot = held[...].reshape(chips * cores * mine, width)
    grad_tokens[...] = lax.dot_general(
        cot, weight[...], (((1,), (1,)), ((), ())), preferred_element_type=F32
    ).astype(BF16)
    grad_weight[...] = lax.dot_general(
        tokens[...], cot, (((0,), (0,)), ((), ())), preferred_element_type=F32
    ).astype(BF16)


def tail_kernel(got, grads, stale, weight, codes, scales, new_weight):
    replicas, twice, width = got.shape
    owned = twice // 2
    total = jnp.sum(got[:, :owned, :].astype(F32), axis=0)
    average = total / replicas
    diagonal = lax.broadcasted_iota(jnp.int32, (owned, owned), 0) == lax.broadcasted_iota(
        jnp.int32, (owned, owned), 1
    )
    for b in range(width // BLOCK):
        columns = slice(b * BLOCK, (b + 1) * BLOCK)
        block = average[:, columns]
        scale = jnp.max(jnp.abs(block), axis=-1, keepdims=True) + EPSILON
        codes[:, columns] = block / scale
        scales[b:b + 1, :] = jnp.sum(jnp.where(diagonal, scale, 0.0), axis=0, keepdims=True)
    change = got[:, owned:, :].astype(F32) + (grads[...].astype(F32) - stale[...].astype(F32)) / replicas
    new_weight[...] = (weight[...].astype(F32) - OUTER_RATE * change).astype(BF16)


def shift(value, axis, k):
    n = lax.axis_size(axis)
    return lax.ppermute(value, axis, [(i, (i + k) % n) for i in range(n)])


def pick(value, index, axis):
    return lax.dynamic_index_in_dim(value, index, axis, False)


def body(pseudo_grad, stale_avg, momentum, weight, tokens, cotangent):
    replicas = lax.axis_size("z") * lax.axis_size("yh")
    runs, line = lax.axis_size("yl"), lax.axis_size("x")
    chips = runs * line
    core, x_at, yl_at = lax.axis_index("core"), lax.axis_index("x"), lax.axis_index("yl")
    at = jnp.stack([lax.axis_index(REPLICA), core, x_at, yl_at]).astype(jnp.int32)
    owned = momentum.shape[2]
    rows, width = weight.shape
    nblocks = width // BLOCK
    mine = cotangent.shape[0]
    dma = pltpu.SemaphoreType.DMA
    block = rows * width

    (copies,) = call(
        spread_kernel,
        [VMEM],
        [((chips, mine, width), BF16, HBM)],
        4 * cotangent.size * chips,
        0,
        [dma((chips,))],
    )(cotangent)
    cot_mine = lax.all_to_all(copies, CHIPS, 0, 0)

    grads = pseudo_grad[0].reshape(replicas, owned, width)
    grouped = tokens.reshape(chips, 2, mine, rows)
    sent, moment_next, theirs = call(
        front_kernel,
        [SMEM, HBM, HBM, VMEM, HBM, VMEM],
        [
            ((replicas, 2 * owned, width), BF16, HBM),
            ((owned, width), F32, VMEM),
            ((chips * mine, width), F32, VMEM),
        ],
        12 * block,
        0,
        [
            pltpu.VMEM((owned, width), BF16),
            pltpu.VMEM((replicas, owned, width), BF16),
            pltpu.VMEM((chips, mine, rows), BF16),
            dma((4,)),
        ],
    )(at, grads, stale_avg, momentum[0, 0], grouped, weight)
    arrived = shift(theirs, "core", 1).reshape(chips, mine, width)
    got = lax.all_to_all(sent, REPLICA, 0, 0)

    arrived, cot_mine = lax.optimization_barrier((arrived, cot_mine))
    kept, *pieces = call(
        own_kernel,
        [SMEM, VMEM, VMEM, VMEM],
        [((runs, mine, width), F32, VMEM)] * line,
        10 * block,
        0,
    )(at, grouped, weight, arrived)
    from_x = [shift(pieces[k - 1], "x", k) for k in (2, 1, 3)]

    cot_theirs = shift(cot_mine, "core", 1)
    grad_tokens, grad_weight = call(
        grads_kernel,
        [SMEM, VMEM, VMEM, HBM, HBM],
        [(tokens.shape, BF16, VMEM), ((rows, width), BF16, VMEM)],
        12 * block,
        0,
        [pltpu.VMEM(grouped.shape, BF16), dma((2,))],
        16 * MIB,
    )(at, tokens, weight, cot_mine, cot_theirs)

    from_x, grad_weight, grad_tokens = lax.optimization_barrier((from_x, grad_weight, grad_tokens))
    acc = kept + from_x[0] + from_x[1] + from_x[2]
    there = shift(pick(acc, 1 - yl_at, 0), "yl", 1)

    codes, scales, new_weight = call(
        tail_kernel,
        [VMEM] * 4,
        [
            ((owned, width), F32, VMEM),
            ((nblocks, owned), F32, VMEM),
            ((replicas, owned, width), BF16, VMEM),
        ],
        12 * block,
        0,
        limit=12 * MIB,
    )(got, grads, stale_avg.reshape(grads.shape), weight.reshape(grads.shape))
    codes, there = lax.optimization_barrier((codes, there))
    keys = (pick(acc, yl_at, 0) + there).astype(BF16)
    return (
        codes[None, None],
        scales.T[None, None],
        moment_next[None, None],
        new_weight.reshape(pseudo_grad.shape),
        keys,
        grad_tokens,
        grad_weight[None],
    )


def solution(mesh):
    fine = Mesh(mesh.devices.reshape(SIZES), REPLICA + TENSOR)
    return jax.shard_map(
        body,
        mesh=fine,
        in_specs=(
            P(REPLICA, TENSOR, None),
            P(TENSOR, None),
            P(TENSOR, REPLICA, None, None),
            P(TENSOR, None),
            P(REPLICA, TENSOR),
            P(REPLICA + TENSOR, None),
        ),
        out_specs=(
            P(TENSOR, REPLICA, None, None),
            P(TENSOR, REPLICA, None, None),
            P(TENSOR, REPLICA, None, None),
            P(REPLICA, TENSOR, None),
            P(REPLICA + TENSOR, None),
            P(REPLICA, TENSOR),
            P(REPLICA, TENSOR, None),
        ),
        check_vma=False,
    )
```

```python
import jax
import jax.numpy as jnp
from jax import lax
from jax.experimental import pallas as pl
from jax.experimental.pallas import tpu as pltpu
from jax.sharding import Mesh, PartitionSpec as P

BLOCK = 128
OUTER_RATE = 0.7
MOMENTUM_COEF = 0.9
EPSILON = 1e-06

REPLICA = ("z", "yh")
TENSOR = ("yl", "x", "core")
CHIPS = ("yl", "x")
SIZES = (8, 4, 2, 4, 2)

MIB = 1024 * 1024
VMEM = pl.BlockSpec(memory_space=pltpu.VMEM)
SMEM = pl.BlockSpec(memory_space=pltpu.SMEM)
HBM = pl.BlockSpec(memory_space=pltpu.HBM)
F32, BF16 = jnp.float32, jnp.bfloat16
struct = jax.ShapeDtypeStruct


def call(kernel, ins, outs, moved, flops, scratch=(), limit=8 * MIB):
    return pl.pallas_call(
        kernel,
        out_shape=[struct(shape, dtype) for shape, dtype, _ in outs],
        in_specs=ins,
        out_specs=[spec for _, _, spec in outs],
        scratch_shapes=list(scratch),
        compiler_params=pltpu.CompilerParams(vmem_limit_bytes=limit),
        cost_estimate=pl.CostEstimate(flops=flops, bytes_accessed=moved, transcendentals=0),
    )


def spread_kernel(rows, out, sems):
    copies = [pltpu.make_async_copy(rows, out.at[i], sems.at[i]) for i in range(out.shape[0])]
    for copy in copies:
        copy.start()
    for copy in copies:
        copy.wait()


def front_kernel(at, grads, stale, momentum, tokens, weight, sent, moment_next, theirs, rows, step, other, sems):
    owned = momentum.shape[0]
    chips, mine, width = other.shape
    copy_rows = pltpu.make_async_copy(
        stale.at[pl.ds(pl.multiple_of(at[0] * owned, owned), owned), :], rows, sems.at[0]
    )
    copy_tokens = pltpu.make_async_copy(tokens.at[:, 1 - at[1]], other, sems.at[1])
    copy_grads = pltpu.make_async_copy(grads, sent.at[:, :owned, :], sems.at[2])
    copy_step = pltpu.make_async_copy(step, sent.at[:, owned:, :], sems.at[3])
    copy_rows.start()
    copy_tokens.start()
    copy_grads.start()
    copy_rows.wait()
    old = rows[...].astype(F32)
    moment = MOMENTUM_COEF * momentum[...] + old
    moment_next[...] = moment
    step[...] = jnp.broadcast_to((old + MOMENTUM_COEF * moment).astype(BF16)[None], step.shape)
    copy_step.start()
    copy_tokens.wait()
    theirs[...] = jnp.dot(
        other[...].reshape(chips * mine, width), weight[...], preferred_element_type=F32
    )
    copy_grads.wait()
    copy_step.wait()


def own_kernel(at, tokens, weight, arrived, *outs):
    runs, mine, width = outs[0].shape
    line = len(outs)
    for k, out in enumerate(outs):
        x = lax.rem(at[2] + k, line)
        rows = jnp.concatenate([tokens[y * line + x, at[1]] for y in range(runs)], axis=0)
        part = jnp.dot(rows, weight[...], preferred_element_type=F32)
        for y in range(runs):
            out[y] = part[y * mine:(y + 1) * mine] + arrived[y * line + x]


def grads_kernel(at, tokens, weight, cot_mine, cot_theirs, grad_tokens, grad_weight, held, sems):
    chips, cores, mine, width = held.shape
    copies = [
        pltpu.make_async_copy(cot_mine, held.at[:, at[1]], sems.at[0]),
        pltpu.make_async_copy(cot_theirs, held.at[:, 1 - at[1]], sems.at[1]),
    ]
    for copy in copies:
        copy.start()
    for copy in copies:
        copy.wait()
    cot = held[...].reshape(chips * cores * mine, width)
    grad_tokens[...] = lax.dot_general(
        cot, weight[...], (((1,), (1,)), ((), ())), preferred_element_type=F32
    ).astype(BF16)
    grad_weight[...] = lax.dot_general(
        tokens[...], cot, (((0,), (0,)), ((), ())), preferred_element_type=F32
    ).astype(BF16)


def tail_kernel(got, grads, stale, weight, here, there, codes, scales, new_weight, keys):
    replicas, twice, width = got.shape
    owned = twice // 2
    total = jnp.sum(got[:, :owned, :].astype(F32), axis=0)
    average = total / replicas
    diagonal = lax.broadcasted_iota(jnp.int32, (owned, owned), 0) == lax.broadcasted_iota(
        jnp.int32, (owned, owned), 1
    )
    for b in range(width // BLOCK):
        columns = slice(b * BLOCK, (b + 1) * BLOCK)
        block = average[:, columns]
        scale = jnp.max(jnp.abs(block), axis=-1, keepdims=True) + EPSILON
        codes[:, columns] = block / scale
        scales[b:b + 1, :] = jnp.sum(jnp.where(diagonal, scale, 0.0), axis=0, keepdims=True)
    change = got[:, owned:, :].astype(F32) + (grads[...].astype(F32) - stale[...].astype(F32)) / replicas
    new_weight[...] = (weight[...].astype(F32) - OUTER_RATE * change).astype(BF16)
    keys[...] = (here[...] + there[...]).astype(BF16)


def shift(value, axis, k):
    n = lax.axis_size(axis)
    return lax.ppermute(value, axis, [(i, (i + k) % n) for i in range(n)])


def pick(value, index, axis):
    return lax.dynamic_index_in_dim(value, index, axis, False)


def body(pseudo_grad, stale_avg, momentum, weight, tokens, cotangent):
    replicas = lax.axis_size("z") * lax.axis_size("yh")
    runs, line = lax.axis_size("yl"), lax.axis_size("x")
    chips = runs * line
    core, x_at, yl_at = lax.axis_index("core"), lax.axis_index("x"), lax.axis_index("yl")
    at = jnp.stack([lax.axis_index(REPLICA), core, x_at, yl_at]).astype(jnp.int32)
    owned = momentum.shape[2]
    rows, width = weight.shape
    nblocks = width // BLOCK
    mine = cotangent.shape[0]
    dma = pltpu.SemaphoreType.DMA
    block = rows * width

    (copies,) = call(
        spread_kernel,
        [VMEM],
        [((chips, mine, width), BF16, HBM)],
        4 * cotangent.size * chips,
        0,
        [dma((chips,))],
    )(cotangent)
    cot_mine = lax.all_to_all(copies, CHIPS, 0, 0)

    grads = pseudo_grad[0].reshape(replicas, owned, width)
    grouped = tokens.reshape(chips, 2, mine, rows)
    sent, moment_next, theirs = call(
        front_kernel,
        [SMEM, HBM, HBM, VMEM, HBM, VMEM],
        [
            ((replicas, 2 * owned, width), BF16, HBM),
            ((owned, width), F32, VMEM),
            ((chips * mine, width), F32, VMEM),
        ],
        12 * block,
        0,
        [
            pltpu.VMEM((owned, width), BF16),
            pltpu.VMEM((replicas, owned, width), BF16),
            pltpu.VMEM((chips, mine, rows), BF16),
            dma((4,)),
        ],
    )(at, grads, stale_avg, momentum[0, 0], grouped, weight)
    arrived = shift(theirs, "core", 1).reshape(chips, mine, width)
    got = lax.all_to_all(sent, REPLICA, 0, 0)

    arrived, cot_mine = lax.optimization_barrier((arrived, cot_mine))
    kept, *pieces = call(
        own_kernel,
        [SMEM, VMEM, VMEM, VMEM],
        [((runs, mine, width), F32, VMEM)] * line,
        10 * block,
        0,
    )(at, grouped, weight, arrived)
    from_x = [shift(pieces[k - 1], "x", k) for k in (2, 1, 3)]

    kept, cot_mine = lax.optimization_barrier((kept, cot_mine))
    cot_theirs = shift(cot_mine, "core", 1)
    grad_tokens, grad_weight = call(
        grads_kernel,
        [SMEM, VMEM, VMEM, HBM, HBM],
        [(tokens.shape, BF16, VMEM), ((rows, width), BF16, VMEM)],
        12 * block,
        0,
        [pltpu.VMEM(grouped.shape, BF16), dma((2,))],
        16 * MIB,
    )(at, tokens, weight, cot_mine, cot_theirs)

    from_x, grad_weight, grad_tokens = lax.optimization_barrier((from_x, grad_weight, grad_tokens))
    acc = kept + from_x[0] + from_x[1] + from_x[2]
    there = shift(pick(acc, 1 - yl_at, 0), "yl", 1)

    codes, scales, new_weight, keys = call(
        tail_kernel,
        [VMEM] * 6,
        [
            ((owned, width), F32, VMEM),
            ((nblocks, owned), F32, VMEM),
            ((replicas, owned, width), BF16, VMEM),
            ((mine, width), BF16, VMEM),
        ],
        12 * block,
        0,
        limit=12 * MIB,
    )(got, grads, stale_avg.reshape(grads.shape), weight.reshape(grads.shape), pick(acc, yl_at, 0), there)
    return (
        codes[None, None],
        scales.T[None, None],
        moment_next[None, None],
        new_weight.reshape(pseudo_grad.shape),
        keys,
        grad_tokens,
        grad_weight[None],
    )


def solution(mesh):
    fine = Mesh(mesh.devices.reshape(SIZES), REPLICA + TENSOR)
    return jax.shard_map(
        body,
        mesh=fine,
        in_specs=(
            P(REPLICA, TENSOR, None),
            P(TENSOR, None),
            P(TENSOR, REPLICA, None, None),
            P(TENSOR, None),
            P(REPLICA, TENSOR),
            P(REPLICA + TENSOR, None),
        ),
        out_specs=(
            P(TENSOR, REPLICA, None, None),
            P(TENSOR, REPLICA, None, None),
            P(TENSOR, REPLICA, None, None),
            P(REPLICA, TENSOR, None),
            P(REPLICA + TENSOR, None),
            P(REPLICA, TENSOR),
            P(REPLICA, TENSOR, None),
        ),
        check_vma=False,
    )
```

```python
import jax
import jax.numpy as jnp
from jax import lax
from jax.experimental import pallas as pl
from jax.experimental.pallas import tpu as pltpu
from jax.sharding import Mesh, PartitionSpec as P

BLOCK = 128
OUTER_RATE = 0.7
MOMENTUM_COEF = 0.9
EPSILON = 1e-06

REPLICA = ("z", "yh")
TENSOR = ("yl", "x", "core")
CHIPS = ("yl", "x")
SIZES = (8, 4, 2, 4, 2)

MIB = 1024 * 1024
VMEM = pl.BlockSpec(memory_space=pltpu.VMEM)
SMEM = pl.BlockSpec(memory_space=pltpu.SMEM)
HBM = pl.BlockSpec(memory_space=pltpu.HBM)
F32, BF16 = jnp.float32, jnp.bfloat16
struct = jax.ShapeDtypeStruct


def call(kernel, ins, outs, moved, flops, scratch=(), limit=8 * MIB):
    return pl.pallas_call(
        kernel,
        out_shape=[struct(shape, dtype) for shape, dtype, _ in outs],
        in_specs=ins,
        out_specs=[spec for _, _, spec in outs],
        scratch_shapes=list(scratch),
        compiler_params=pltpu.CompilerParams(vmem_limit_bytes=limit),
        cost_estimate=pl.CostEstimate(flops=flops, bytes_accessed=moved, transcendentals=0),
    )


def spread_kernel(rows, out, sems):
    copies = [pltpu.make_async_copy(rows, out.at[i], sems.at[i]) for i in range(out.shape[0])]
    for copy in copies:
        copy.start()
    for copy in copies:
        copy.wait()


def front_kernel(at, grads, stale, momentum, tokens, weight, sent, moment_next, theirs, rows, step, other, sems):
    owned = momentum.shape[0]
    chips, mine, width = other.shape
    copy_rows = pltpu.make_async_copy(
        stale.at[pl.ds(pl.multiple_of(at[0] * owned, owned), owned), :], rows, sems.at[0]
    )
    copy_tokens = pltpu.make_async_copy(tokens.at[:, 1 - at[1]], other, sems.at[1])
    copy_grads = pltpu.make_async_copy(grads, sent.at[:, :owned, :], sems.at[2])
    copy_step = pltpu.make_async_copy(step, sent.at[:, owned:, :], sems.at[3])
    copy_rows.start()
    copy_tokens.start()
    copy_grads.start()
    copy_rows.wait()
    old = rows[...].astype(F32)
    moment = MOMENTUM_COEF * momentum[...] + old
    moment_next[...] = moment
    step[...] = jnp.broadcast_to((old + MOMENTUM_COEF * moment).astype(BF16)[None], step.shape)
    copy_step.start()
    copy_tokens.wait()
    theirs[...] = jnp.dot(
        other[...].reshape(chips * mine, width), weight[...], preferred_element_type=F32
    )
    copy_grads.wait()
    copy_step.wait()


def own_kernel(at, tokens, weight, arrived, *outs):
    runs, mine, width = outs[0].shape
    line = len(outs)
    for k, out in enumerate(outs):
        x = lax.rem(at[2] + k, line)
        rows = jnp.concatenate([tokens[y * line + x, at[1]] for y in range(runs)], axis=0)
        part = jnp.dot(rows, weight[...], preferred_element_type=F32)
        for y in range(runs):
            out[y] = part[y * mine:(y + 1) * mine] + arrived[y * line + x]


def grads_kernel(at, tokens, weight, cot_mine, cot_theirs, grad_tokens, grad_weight, held, sems):
    chips, cores, mine, width = held.shape
    copies = [
        pltpu.make_async_copy(cot_mine, held.at[:, at[1]], sems.at[0]),
        pltpu.make_async_copy(cot_theirs, held.at[:, 1 - at[1]], sems.at[1]),
    ]
    for copy in copies:
        copy.start()
    for copy in copies:
        copy.wait()
    cot = held[...].reshape(chips * cores * mine, width)
    grad_tokens[...] = lax.dot_general(
        cot, weight[...], (((1,), (1,)), ((), ())), preferred_element_type=F32
    ).astype(BF16)
    grad_weight[...] = lax.dot_general(
        tokens[...], cot, (((0,), (0,)), ((), ())), preferred_element_type=F32
    ).astype(BF16)


def tail_kernel(got, grads, stale, weight, codes, scales, new_weight):
    replicas, twice, width = got.shape
    owned = twice // 2
    total = jnp.sum(got[:, :owned, :].astype(F32), axis=0)
    average = total / replicas
    diagonal = lax.broadcasted_iota(jnp.int32, (owned, owned), 0) == lax.broadcasted_iota(
        jnp.int32, (owned, owned), 1
    )
    for b in range(width // BLOCK):
        columns = slice(b * BLOCK, (b + 1) * BLOCK)
        block = average[:, columns]
        scale = jnp.max(jnp.abs(block), axis=-1, keepdims=True) + EPSILON
        codes[:, columns] = block / scale
        scales[b:b + 1, :] = jnp.sum(jnp.where(diagonal, scale, 0.0), axis=0, keepdims=True)
    change = got[:, owned:, :].astype(F32) + (grads[...].astype(F32) - stale[...].astype(F32)) / replicas
    new_weight[...] = (weight[...].astype(F32) - OUTER_RATE * change).astype(BF16)


def shift(value, axis, k):
    n = lax.axis_size(axis)
    return lax.ppermute(value, axis, [(i, (i + k) % n) for i in range(n)])


def pick(value, index, axis):
    return lax.dynamic_index_in_dim(value, index, axis, False)


def body(pseudo_grad, stale_avg, momentum, weight, tokens, cotangent):
    replicas = lax.axis_size("z") * lax.axis_size("yh")
    runs, line = lax.axis_size("yl"), lax.axis_size("x")
    chips = runs * line
    core, x_at, yl_at = lax.axis_index("core"), lax.axis_index("x"), lax.axis_index("yl")
    at = jnp.stack([lax.axis_index(REPLICA), core, x_at, yl_at]).astype(jnp.int32)
    owned = momentum.shape[2]
    rows, width = weight.shape
    nblocks = width // BLOCK
    mine = cotangent.shape[0]
    dma = pltpu.SemaphoreType.DMA
    block = rows * width

    (copies,) = call(
        spread_kernel,
        [VMEM],
        [((chips, mine, width), BF16, HBM)],
        4 * cotangent.size * chips,
        0,
        [dma((chips,))],
    )(cotangent)
    cot_mine = lax.all_to_all(copies, CHIPS, 0, 0)

    grads = pseudo_grad[0].reshape(replicas, owned, width)
    grouped = tokens.reshape(chips, 2, mine, rows)
    sent, moment_next, theirs = call(
        front_kernel,
        [SMEM, HBM, HBM, VMEM, HBM, VMEM],
        [
            ((replicas, 2 * owned, width), BF16, HBM),
            ((owned, width), F32, VMEM),
            ((chips * mine, width), F32, VMEM),
        ],
        12 * block,
        0,
        [
            pltpu.VMEM((owned, width), BF16),
            pltpu.VMEM((replicas, owned, width), BF16),
            pltpu.VMEM((chips, mine, rows), BF16),
            dma((4,)),
        ],
    )(at, grads, stale_avg, momentum[0, 0], grouped, weight)
    arrived = shift(theirs, "core", 1).reshape(chips, mine, width)
    got = lax.all_to_all(sent, REPLICA, 0, 0)

    arrived, cot_mine = lax.optimization_barrier((arrived, cot_mine))
    kept, *pieces = call(
        own_kernel,
        [SMEM, VMEM, VMEM, VMEM],
        [((runs, mine, width), F32, VMEM)] * line,
        10 * block,
        0,
    )(at, grouped, weight, arrived)
    from_x = [shift(pieces[k - 1], "x", k) for k in (2, 1, 3)]

    kept, cot_mine = lax.optimization_barrier((kept, cot_mine))
    cot_theirs = shift(cot_mine, "core", 1)
    grad_tokens, grad_weight = call(
        grads_kernel,
        [SMEM, VMEM, VMEM, HBM, HBM],
        [(tokens.shape, BF16, VMEM), ((rows, width), BF16, VMEM)],
        12 * block,
        0,
        [pltpu.VMEM(grouped.shape, BF16), dma((2,))],
        16 * MIB,
    )(at, tokens, weight, cot_mine, cot_theirs)

    from_x, grad_weight, grad_tokens = lax.optimization_barrier((from_x, grad_weight, grad_tokens))
    acc = kept + from_x[0] + from_x[1] + from_x[2]
    there = shift(pick(acc, 1 - yl_at, 0), "yl", 1)

    codes, scales, new_weight = call(
        tail_kernel,
        [VMEM] * 4,
        [
            ((owned, width), F32, VMEM),
            ((nblocks, owned), F32, VMEM),
            ((replicas, owned, width), BF16, VMEM),
        ],
        12 * block,
        0,
        limit=12 * MIB,
    )(got, grads, stale_avg.reshape(grads.shape), weight.reshape(grads.shape))
    codes, there = lax.optimization_barrier((codes, there))
    keys = (pick(acc, yl_at, 0) + there).astype(BF16)
    return (
        codes[None, None],
        scales.T[None, None],
        moment_next[None, None],
        new_weight.reshape(pseudo_grad.shape),
        keys,
        grad_tokens,
        grad_weight[None],
    )


def solution(mesh):
    fine = Mesh(mesh.devices.reshape(SIZES), REPLICA + TENSOR)
    return jax.shard_map(
        body,
        mesh=fine,
        in_specs=(
            P(REPLICA, TENSOR, None),
            P(TENSOR, None),
            P(TENSOR, REPLICA, None, None),
            P(TENSOR, None),
            P(REPLICA, TENSOR),
            P(REPLICA + TENSOR, None),
        ),
        out_specs=(
            P(TENSOR, REPLICA, None, None),
            P(TENSOR, REPLICA, None, None),
            P(TENSOR, REPLICA, None, None),
            P(REPLICA, TENSOR, None),
            P(REPLICA + TENSOR, None),
            P(REPLICA, TENSOR),
            P(REPLICA, TENSOR, None),
        ),
        check_vma=False,
    )
```
